32 devices in a mesh: tile: 16 (over z, x, core), mode: 2 (over y).
Axes of the slice: x: 2, y: 2, z: 4, core: 2. Of those that a mesh axis runs over, the one named last changes fastest.
Arguments:
- object_field: float32 [2, 4096, 1024], P(None, 'tile'), may hold values from -6 to 6
- probe_modes: float32 [2, 8, 256, 256], P(None, 'mode'), may hold values from -1.5 to 1.5
- measured: float32 [128, 256, 256], P('tile'), may hold values from 0.05 to 4
- row_starts: int32 [128], P('tile'), may hold values from -128 to 128, as said below
- col_starts: int32 [128], P('tile'), may hold values from 0 to 768
- live_counts: int32 [16], P('tile'), may hold values from 1 to 8, 96 in all
Outputs:
- object_grad: float32 [2, 4096, 1024], P(None, 'tile', 'mode')
- probe_grad: float32 [2, 8, 256, 256], P(None, 'mode')
The draws below stay inside these ranges and needn't reach their ends.
Inputs may be any that keep to these rules, and one draw needn't show every extreme that they name: A window lies inside the object: on tile 0 row_starts is at least 0, on the last tile at most 0; elsewhere a window reaches at most 128 rows into the tile above or below. `live_counts`: slots of a tile from its count on are unused.
All inputs are finite; a program needn't handle non-finite values. No bound on the sum of `live_counts` on one device may be relied on, other than what follows from the above.
Results may differ from the reference program's by a relative error of at most 0.0056.
Values sent between devices are 32-bit elements; how exact they have to be, the bound alone decides.
A program may use at most 128 MiB of HBM per device.

```python
import math
import jax
import jax.numpy as jnp
import numpy as np
from jax import lax

WIN = 256
MODES = 8
POS_DEV = 8
TILE_R = 256
OBJ_C = 1024
HALF = 128
N_POS = 128
OBJ_R = 4096
N_TILE = 16


def draw_row_starts(key, part):
    mixed_key = jax.random.fold_in(key, 11)
    devices_count = N_POS // POS_DEV
    slot_index = jnp.arange(N_POS, dtype=jnp.int32)
    owner_tile = slot_index // POS_DEV
    within = slot_index % POS_DEV
    lowest = jnp.where(owner_tile == 0, 0, 0 - HALF)
    highest = jnp.where(owner_tile == devices_count - 1, TILE_R - WIN, TILE_R - HALF)
    random_bits = jax.random.randint(mixed_key, (N_POS,), 0, 1048576, dtype=jnp.int32)
    row_start = lowest + random_bits % (highest - lowest + 1)
    row_start = jnp.where((owner_tile == 1) & (within == 0), 0 - HALF, row_start)
    row_start = jnp.where((owner_tile == 1) & (within == 1), TILE_R - HALF, row_start)
    return row_start.astype(jnp.int32)


def draw_col_starts(key, part):
    mixed_key = jax.random.fold_in(key, 23)
    slot_index = jnp.arange(N_POS, dtype=jnp.int32)
    within = slot_index % POS_DEV
    random_bits = jax.random.randint(mixed_key, (N_POS,), 0, 1048576, dtype=jnp.int32)
    col_start = random_bits % (OBJ_C - WIN + 1)
    col_start = jnp.where(within == 0, 0, col_start)
    col_start = jnp.where(within == 1, OBJ_C - WIN, col_start)
    return col_start.astype(jnp.int32)


def level_of(rng, dims, pieces, low, top_value):
    loudness = 1.0
    for dim, blocks in pieces:
        draws = jax.random.uniform(jax.random.fold_in(jax.random.fold_in(rng, 6), dim), (blocks,), jnp.float32, low / len(pieces), top_value / len(pieces))
        loudness = loudness * jnp.repeat(jnp.exp(draws), dims[dim] // blocks).reshape((-1,) + (1,) * (len(dims) - 1 - dim))
    return loudness


def length_profile(number_of, total, reach, slope):
    portions = [(1 << 20) // math.isqrt(grade ** slope) + 1 for grade in range(2, number_of + 1)]
    spare, holding = total - reach - (number_of - 1), [1] * (number_of - 1)
    while spare > 0:
        candidates = [i for i in range(number_of - 1) if holding[i] < reach]
        mass, budget = sum([portions[i] for i in candidates]), spare
        for i in candidates:
            more = min(reach - holding[i], max(1, budget * portions[i] // mass), spare)
            holding[i] = holding[i] + more
            spare = spare - more
    return np.array([reach] + holding)


def uneven_parts(rng, number_of, total, limit, slope):
    if number_of == 2:
        one = jax.random.randint(rng, (), max(1, total - limit), min(limit, total - 1) + 1)
        return jnp.stack([one, total - one])
    sizes = jnp.asarray(length_profile(number_of, total, limit, slope), jnp.int32)
    couples = (number_of - 1) // 2
    giver, receiver = sizes[1:1 + 2 * couples:2], sizes[2:2 + 2 * couples:2]
    slack = jnp.minimum(giver - 1, limit - receiver)
    passed = jax.random.randint(jax.random.fold_in(rng, 1), (couples,), 0, 1 << 20) % (slack + 1)
    sizes = sizes.at[1:1 + 2 * couples:2].set(giver - passed).at[2:2 + 2 * couples:2].set(receiver + passed)
    return sizes[jax.random.permutation(jax.random.fold_in(rng, 2), number_of)]


def normal_values(key, shape, spread, limit, cuts=(), kind=jnp.bfloat16):
    drawn = jax.random.normal(key, shape, jnp.float32) * spread
    if len(cuts) > 0:
        drawn = level_of(key, shape, cuts, -0.22, 0.18) * drawn
    return jnp.clip(drawn, min=-limit, max=limit).astype(kind)


def setup_inputs(seed: int = 0) -> dict:
    arg_keys = jax.random.split(jax.random.key(seed), 7)
    object_field = normal_values(arg_keys[0], (2, OBJ_R, OBJ_C), 0.7, 6.0, ((1, 16),), jnp.float32)
    probe_modes = normal_values(arg_keys[1], (2, MODES, WIN, WIN), (2 * MODES) ** -0.5, 1.5, ((1, 2),), jnp.float32)
    measured = jnp.clip(jnp.exp(math.log(4.0) - 4.3820266 * jax.random.uniform(arg_keys[2], (N_POS, WIN, WIN), jnp.float32) ** level_of(arg_keys[2], (N_POS, WIN, WIN), ((0, 16),), -0.2, 0.2)), 0.05, 4.0)
    row_starts = draw_row_starts(jax.random.fold_in(arg_keys[6], 71), 0)
    col_starts = draw_col_starts(jax.random.fold_in(arg_keys[6], 71), 0)
    live_counts = uneven_parts(arg_keys[5], N_TILE, N_POS * 3 // 4, POS_DEV, 2).astype(jnp.int32)
    return dict(object_field=object_field, probe_modes=probe_modes, measured=measured, row_starts=row_starts, col_starts=col_starts, live_counts=live_counts)


def dft_blocks(window, conj_sign):
    index_range = jnp.arange(window, dtype=jnp.int32)
    phases = index_range[:, None] * index_range[None, :] % window
    angles = phases.astype(jnp.float32) * (-2.0 * math.pi / window)
    norm_scale = 1.0 / math.sqrt(window)
    cosine_table = (jnp.cos(angles) * norm_scale).astype(jnp.bfloat16)
    sine_table = (jnp.sin(angles) * (norm_scale * conj_sign)).astype(jnp.bfloat16)
    return jnp.stack([jnp.stack([cosine_table, -sine_table]), jnp.stack([sine_table, cosine_table])])

def transform(wave_field, blocks_table):
    table_wide = blocks_table.astype(jnp.float32)
    half_pass = jnp.einsum('abkr,bpmrc->apmkc', table_wide, wave_field.astype(jnp.float32), precision=lax.Precision.HIGHEST)
    half_pass = lax.optimization_barrier(half_pass.astype(jnp.bfloat16)).astype(jnp.float32)
    return jnp.einsum('bpmrc,abck->apmrk', half_pass, table_wide, precision=lax.Precision.HIGHEST)

def complex_times(left_factor, right_factor):
    return jnp.stack([left_factor[0] * right_factor[0] - left_factor[1] * right_factor[1], left_factor[0] * right_factor[1] + left_factor[1] * right_factor[0]])

def conj_times(left_factor, right_factor):
    return jnp.stack([left_factor[0] * right_factor[0] + left_factor[1] * right_factor[1], left_factor[0] * right_factor[1] - left_factor[1] * right_factor[0]])

def amplitude_scaling(model_intensity, measured_block, live_block):
    floored = jnp.maximum(jnp.sqrt(model_intensity), 0.5)
    return live_block[:, None, None] * (1.0 - jnp.sqrt(measured_block) / floored)

def place_terms(accumulated, terms, row_tops, col_lefts):
    window = terms.shape[-1]
    zero_index = jnp.zeros((), jnp.int32)

    def place_one(position, current):
        anchor = (zero_index, row_tops[position], col_lefts[position])
        old_values = lax.dynamic_slice(current, anchor, (2, window, window))
        return lax.dynamic_update_slice(current, old_values + terms[:, position], anchor)
    return lax.fori_loop(0, terms.shape[1], place_one, accumulated)

def reference(object_field, probe_modes, measured, row_starts, col_starts, live_counts):
    forward_blocks = dft_blocks(WIN, 1.0)
    backward_blocks = dft_blocks(WIN, -1.0)
    slot_index = jnp.arange(N_POS, dtype=jnp.int32)
    owner_tile = slot_index // POS_DEV
    row_tops = (owner_tile * TILE_R + row_starts).astype(jnp.int32)
    live_mask = (slot_index % POS_DEV < live_counts[owner_tile]).astype(jnp.float32)
    tiles_count = N_POS // POS_DEV
    tile_items = (row_tops.reshape(tiles_count, POS_DEV), col_starts.astype(jnp.int32).reshape(tiles_count, POS_DEV), live_mask.reshape(tiles_count, POS_DEV), measured.reshape(tiles_count, POS_DEV, WIN, WIN))

    def take_patch(row_top, col_left):
        zero_index = jnp.zeros((), jnp.int32)
        return lax.dynamic_slice(object_field, (zero_index, row_top, col_left), (2, WIN, WIN))

    def advance(running, items_now):
        object_grad, probe_grad = running
        tile_tops, tile_lefts, tile_live, tile_measured = items_now
        patches = jax.vmap(take_patch, in_axes=(0, 0), out_axes=1)(tile_tops, tile_lefts)
        exit_wave = lax.optimization_barrier(complex_times(probe_modes[:, None], patches[:, :, None]).astype(jnp.bfloat16))
        far_field = transform(exit_wave, forward_blocks)
        model_intensity = lax.optimization_barrier(jnp.sum(far_field[0] * far_field[0] + far_field[1] * far_field[1], axis=1))
        scaling = amplitude_scaling(model_intensity, tile_measured, tile_live)
        residual_wave = lax.optimization_barrier((far_field * scaling[None, :, None]).astype(jnp.bfloat16))
        back_wave = transform(residual_wave, backward_blocks)
        object_terms = lax.optimization_barrier(jnp.sum(conj_times(probe_modes[:, None], back_wave), axis=2))
        probe_grad = probe_grad + lax.optimization_barrier(jnp.sum(conj_times(patches[:, :, None], back_wave), axis=1))
        object_grad = place_terms(object_grad, object_terms, tile_tops, tile_lefts)
        return ((object_grad, probe_grad), None)
    start_state = (jnp.zeros(object_field.shape, jnp.float32), jnp.zeros(probe_modes.shape, jnp.float32))
    final_state, unused_out = lax.scan(advance, start_state, tile_items)
    return (final_state[0], final_state[1])
```

```python
import functools
import math

import jax
import jax.numpy as jnp
import numpy as np
from jax import lax
from jax.experimental import pallas as pl
from jax.experimental.pallas import tpu as pltpu
from jax.sharding import PartitionSpec as P

MESH = pl.DeviceIdType.MESH
MIB = 1024 * 1024
F32 = jnp.float32
BF16 = jnp.bfloat16


def dft_tables(window):
    index = np.arange(window)
    angles = (index[:, None] * index[None, :] % window) * (2.0 * math.pi / window)
    cr = np.cos(angles) / math.sqrt(window)
    ci = -np.sin(angles) / math.sqrt(window)
    left = np.block([[cr, -ci], [ci, cr]])
    right = np.block([[cr, ci], [-ci, cr]])
    return jnp.asarray(left, BF16), jnp.asarray(right, BF16)


def gather_kernel(tiles, peers, half, obj, prb, above, below, allp, halo_s, halo_r, prb_s, prb_r, fwd_s, fwd_r, loc):
    t = lax.axis_index("tile")
    m = lax.axis_index("mode")
    sib = t + 1 - 2 * (t % 2)
    c = t % 2
    tile_rows = obj.shape[1]
    nm = prb.shape[1]
    win = prb.shape[2]
    hw = win // 2
    barrier = pltpu.get_barrier_semaphore()

    def hello(tt, mm):
        pl.semaphore_signal(barrier, inc=1, device_id=(tt, mm), device_id_type=MESH)

    @pl.when(t > 0)
    def _():
        hello(t - 1, m)

    @pl.when(t < tiles - 1)
    def _():
        hello(t + 1, m)

    for d in range(1, peers):
        hello(t, (m + d) % peers)
    pl.semaphore_wait(barrier, peers - 1 + (t + tiles - 1) // tiles + (2 * tiles - 2 - t) // tiles)

    own = pltpu.make_async_copy(prb, allp.at[:, pl.ds(m * nm, nm)], loc)

    def probe_copy(d, part):
        return pltpu.make_async_remote_copy(
            src_ref=prb.at[part, :, pl.ds(c * hw, hw)],
            dst_ref=allp.at[part, pl.ds(m * nm, nm), pl.ds(c * hw, hw)],
            send_sem=prb_s.at[d - 1, part],
            recv_sem=prb_r.at[d - 1, part],
            device_id=(t, (m + d) % peers),
            device_id_type=MESH,
        )

    def forward_copy(d, part, core):
        src = (m - d + peers) % peers
        view = allp.at[part, pl.ds(src * nm, nm), pl.ds(core * hw, hw)]
        return pltpu.make_async_remote_copy(
            src_ref=view,
            dst_ref=view,
            send_sem=fwd_s.at[d - 1, part],
            recv_sem=fwd_r.at[d - 1, part],
            device_id=(sib, m),
            device_id_type=MESH,
        )

    up = pltpu.make_async_remote_copy(
        src_ref=obj.at[:, pl.ds(tile_rows - half, half)], dst_ref=above,
        send_sem=halo_s.at[0], recv_sem=halo_r.at[0], device_id=(t + 1, m), device_id_type=MESH)
    down = pltpu.make_async_remote_copy(
        src_ref=obj.at[:, pl.ds(0, half)], dst_ref=below,
        send_sem=halo_s.at[1], recv_sem=halo_r.at[1], device_id=(t - 1, m), device_id_type=MESH)

    @pl.when(t < tiles - 1)
    def _():
        up.start()

    @pl.when(t > 0)
    def _():
        down.start()

    for d in range(1, peers):
        for part in range(2):
            probe_copy(d, part).start()
    own.start()
    for d in range(1, peers):
        for part in range(2):
            probe_copy(d, part).wait_recv()
            forward_copy(d, part, c).start()
    for d in range(1, peers):
        for part in range(2):
            forward_copy(d, part, 1 - c).wait_recv()
            forward_copy(d, part, c).wait_send()
            probe_copy(d, part).wait_send()
    own.wait()

    @pl.when(t > 0)
    def _():
        up.wait_recv()
        down.wait_send()

    @pl.when(t < tiles - 1)
    def _():
        down.wait_recv()
        up.wait_send()


def gather(obj, prb, tiles, peers, half):
    cols = obj.shape[2]
    nm, win = prb.shape[1:3]
    dma = pltpu.SemaphoreType.DMA
    anyspace = pl.BlockSpec(memory_space=pl.ANY)
    return pl.pallas_call(
        functools.partial(gather_kernel, tiles, peers, half),
        out_shape=(
            jax.ShapeDtypeStruct((2, half, cols), F32),
            jax.ShapeDtypeStruct((2, half, cols), F32),
            jax.ShapeDtypeStruct((2, nm * peers, win, win), F32),
        ),
        in_specs=[anyspace, anyspace],
        out_specs=(anyspace, anyspace, anyspace),
        scratch_shapes=[dma((2,)), dma((2,)), dma((peers - 1, 2)), dma((peers - 1, 2)),
                        dma((peers - 1, 2)), dma((peers - 1, 2)), dma],
        compiler_params=pltpu.CompilerParams(collective_id=1, has_side_effects=True),
    )(obj, prb)


def compute_kernel(half, rows, cols, live, me, above, obj, below, prb, measured, left, right,
                   grad, pgrad, padded, far, patch, terms, meas, sems):
    peers = me[1]
    m = me[0]
    win = patch.shape[1]
    tile_rows = obj.shape[1]
    modes = prb.shape[1]
    copies = [
        pltpu.make_async_copy(above, padded.at[:, pl.ds(0, half)], sems.at[0]),
        pltpu.make_async_copy(obj, padded.at[:, pl.ds(half, tile_rows)], sems.at[1]),
        pltpu.make_async_copy(below, padded.at[:, pl.ds(half + tile_rows, half)], sems.at[2]),
    ]
    for copy in copies:
        copy.start()
    grad[...] = jnp.zeros(grad.shape, F32)
    pgrad[...] = jnp.zeros(pgrad.shape, F32)
    for copy in copies:
        copy.wait()
    count = (live[0] - m + peers - 1) // peers

    def position(i, carry):
        slot = m + i * peers
        fetch = pltpu.make_async_copy(measured.at[slot], meas.at[0], sems.at[3])
        fetch.start()
        row = rows[slot] + half
        col = cols[slot]
        base = pl.multiple_of(jnp.minimum(col // 128, (padded.shape[2] - win - 128) // 128) * 128, 128)
        shift = col - base
        wide = win + 128
        tall = win + 8
        top = pl.multiple_of(jnp.minimum(row // 8, (padded.shape[1] - tall) // 8) * 8, 8)
        drop = row - top
        for part in range(2):
            block = padded[part, pl.ds(top, tall), pl.ds(base, wide)]
            block = pltpu.roll(block, (tall - drop) % tall, 0)[:win]
            patch[part] = pltpu.roll(block, (wide - shift) % wide, 1)[:, :win]
        meas[1] = jnp.zeros((win, win), F32)

        def forward(pair, carry):
            pr, pi = patch[0], patch[1]
            exits = []
            for k in range(2):
                qr, qi = prb[0, 2 * pair + k], prb[1, 2 * pair + k]
                er = (qr * pr - qi * pi).astype(BF16)
                ei = (qr * pi + qi * pr).astype(BF16)
                exits.append(jnp.concatenate([er, ei], axis=0))
            wave = jnp.concatenate(exits, axis=1)
            halfp = jnp.dot(left[...], wave, preferred_element_type=F32).astype(BF16)
            for k in range(2):
                lhs = jnp.concatenate(
                    [halfp[:win, k * win:(k + 1) * win], halfp[win:, k * win:(k + 1) * win]], axis=1)
                out = jnp.dot(lhs, right[...], preferred_element_type=F32)
                far[2 * pair + k] = out
                fr, fi = out[:, :win], out[:, win:]
                meas[1] += fr * fr + fi * fi
            return carry

        lax.fori_loop(0, modes // 2, forward, 0)
        fetch.wait()
        meas[1] = 1.0 - jnp.sqrt(meas[0]) / jnp.maximum(jnp.sqrt(meas[1]), 0.5)
        terms[...] = jnp.zeros(terms.shape, F32)

        def backward(pair, carry):
            scaling = meas[1]
            chis = []
            for k in range(2):
                value = far[2 * pair + k]
                chis.append(jnp.concatenate(
                    [(value[:, :win] * scaling).astype(BF16), (value[:, win:] * scaling).astype(BF16)], axis=0))
            wave = jnp.concatenate(chis, axis=1)
            halfp = jnp.dot(right[...], wave, preferred_element_type=F32).astype(BF16)
            for k in range(2):
                mode = 2 * pair + k
                lhs = jnp.concatenate(
                    [halfp[:win, k * win:(k + 1) * win], halfp[win:, k * win:(k + 1) * win]], axis=1)
                back = jnp.dot(lhs, left[...], preferred_element_type=F32)
                br, bi = back[:, :win], back[:, win:]
                pr, pi = patch[0], patch[1]
                qr, qi = prb[0, mode], prb[1, mode]
                terms[0, :win, :win] += qr * br + qi * bi
                terms[1, :win, :win] += qr * bi - qi * br
                pgrad[0, mode] += pr * br + pi * bi
                pgrad[1, mode] += pr * bi - pi * br
            return carry

        lax.fori_loop(0, modes // 2, backward, 0)
        for part in range(2):
            grad[part, pl.ds(top, tall), pl.ds(base, wide)] += pltpu.roll(pltpu.roll(terms[part], shift, 1), drop, 0)
        return carry

    lax.fori_loop(0, count, position, 0)


def compute(rows, cols, live, me, above, obj, below, prb, measured, half):
    win = prb.shape[2]
    modes = prb.shape[1]
    left, right = dft_tables(win)
    anyspace = pl.BlockSpec(memory_space=pl.ANY)
    smem = pl.BlockSpec(memory_space=pltpu.SMEM)
    vmem = pl.BlockSpec(memory_space=pltpu.VMEM)
    height = obj.shape[1] + 2 * half
    return pl.pallas_call(
        functools.partial(compute_kernel, half),
        out_shape=(
            jax.ShapeDtypeStruct((2, height, obj.shape[2]), F32),
            jax.ShapeDtypeStruct(prb.shape, F32),
        ),
        in_specs=[smem, smem, smem, smem, anyspace, anyspace, anyspace, vmem, anyspace, vmem, vmem],
        out_specs=(vmem, vmem),
        scratch_shapes=[
            pltpu.VMEM((2, height, obj.shape[2]), F32),
            pltpu.VMEM((modes, win, 2 * win), F32),
            pltpu.VMEM((2, win, win), F32),
            pltpu.VMEM((2, win + 8, win + 128), F32),
            pltpu.VMEM((2, win, win), F32),
            pltpu.SemaphoreType.DMA((4,)),
        ],
        compiler_params=pltpu.CompilerParams(vmem_limit_bytes=48 * MIB),
    )(rows, cols, live, me, above, obj, below, prb, measured, left, right)


def reduce_kernel(tiles, peers, half, grad, pgrad, ograd, oprobe,
                  edge, sibp, modep, mine, chipp, objp,
                  edge_s, edge_r, sib_s, sib_r, mode_s, mode_r, chip_s, chip_r, obj_s, obj_r, ag_s, ag_r, fw_s, fw_r):
    t = lax.axis_index("tile")
    m = lax.axis_index("mode")
    c = t % 2
    q = t // 2
    chips = tiles // 2
    sib = t + 1 - 2 * c
    modes, win = pgrad.shape[1:3]
    nm = modes // peers
    hw = win // 2
    tile_rows = ograd.shape[1]
    width = ograd.shape[2]
    rows = hw // chips
    barrier = pltpu.get_barrier_semaphore()

    def hello(tt, mm):
        pl.semaphore_signal(barrier, inc=1, device_id=(tt, mm), device_id_type=MESH)

    def chip_tile(d):
        return ((q + d) % chips) * 2 + c

    @pl.when(t > 0)
    def _():
        hello(t - 1, m)

    @pl.when(t < tiles - 1)
    def _():
        hello(t + 1, m)

    for d in range(1, peers):
        hello(t, (m + d) % peers)
    for d in range(1, chips):
        hello(chip_tile(d), m)
    pl.semaphore_wait(barrier, peers + chips - 2 + (t + tiles - 1) // tiles + (2 * tiles - 2 - t) // tiles)

    def remote(src, dst, ssem, rsem, tt, mm):
        return pltpu.make_async_remote_copy(
            src_ref=src, dst_ref=dst, send_sem=ssem, recv_sem=rsem,
            device_id=(tt, mm), device_id_type=MESH)

    to_next = remote(grad.at[:, pl.ds(half + tile_rows, half)], edge.at[0], edge_s.at[0], edge_r.at[0], t + 1, m)
    to_prev = remote(grad.at[:, pl.ds(0, half)], edge.at[1], edge_s.at[1], edge_r.at[1], t - 1, m)

    def sib_copy(d):
        group = ((m + d) % peers) * nm
        return remote(pgrad.at[:, pl.ds(group, nm), pl.ds((1 - c) * hw, hw)], sibp.at[d],
                      sib_s.at[d], sib_r.at[d], sib, m)

    def mode_copy(d):
        return remote(sibp.at[d], modep.at[d - 1], mode_s.at[d - 1], mode_r.at[d - 1], t, (m + d) % peers)

    def chip_copy(d):
        k = (q + d) % chips
        return remote(mine.at[:, :, pl.ds(k * rows, rows)], chipp.at[d - 1],
                      chip_s.at[d - 1], chip_r.at[d - 1], chip_tile(d), m)

    def obj_copy(d, upper):
        column = ((m + d) % peers) * width
        hr = tile_rows // 2
        return remote(grad.at[:, pl.ds(half + upper * hr, hr), pl.ds(column, width)],
                      objp.at[d - 1, :, pl.ds(upper * hr, hr)],
                      obj_s.at[d - 1, upper], obj_r.at[d - 1, upper], t, (m + d) % peers)

    def out_view(core, chip):
        return oprobe.at[:, :, pl.ds(core * hw + chip * rows, rows)]

    def ag_copy(d):
        return remote(out_view(c, q), out_view(c, q), ag_s.at[d - 1], ag_r.at[d - 1], chip_tile(d), m)

    def fw_copy(d, core):
        chip = (q - d + chips) % chips
        return remote(out_view(core, chip), out_view(core, chip), fw_s.at[d], fw_r.at[d], sib, m)

    for d in list(range(1, peers)) + [0]:
        sib_copy(d).start()

    @pl.when(t < tiles - 1)
    def _():
        to_next.start()

    @pl.when(t > 0)
    def _():
        to_prev.start()

    for d in range(1, peers):
        group = ((m + d) % peers) * nm
        sib_copy(d).wait_recv()
        sibp[d] += pgrad[:, pl.ds(group, nm), pl.ds(c * hw, hw)]
        mode_copy(d).start()
    sib_copy(0).wait_recv()
    mine[...] = sibp[0] + pgrad[:, pl.ds(m * nm, nm), pl.ds(c * hw, hw)]

    @pl.when(t > 0)
    def _():
        to_next.wait_recv()
        grad[:, pl.ds(half, half)] += edge[0]

    for d in range(1, peers):
        obj_copy(d, 0).start()

    @pl.when(t < tiles - 1)
    def _():
        to_prev.wait_recv()
        grad[:, pl.ds(tile_rows, half)] += edge[1]

    for d in range(1, peers):
        obj_copy(d, 1).start()
    for d in range(1, peers):
        mode_copy(d).wait_recv()
        mine[...] += modep[d - 1]
    for d in range(1, chips):
        chip_copy(d).start()
    total = mine[:, :, pl.ds(q * rows, rows)]
    for d in range(1, chips):
        chip_copy(d).wait_recv()
        total += chipp[d - 1]
    oprobe[:, :, pl.ds(c * hw + q * rows, rows)] = total
    for d in range(1, chips):
        ag_copy(d).start()
    fw_copy(0, c).start()
    for d in range(1, chips):
        ag_copy(d).wait_recv()
        fw_copy(d, c).start()

    ograd[...] = grad[:, pl.ds(half, tile_rows), pl.ds(pl.multiple_of(m * width, 128), width)]
    for d in range(1, peers):
        for upper in range(2):
            obj_copy(d, upper).wait_recv()
        ograd[...] += objp[d - 1]
    for d in range(chips):
        fw_copy(d, 1 - c).wait_recv()
        fw_copy(d, c).wait_send()

    @pl.when(t < tiles - 1)
    def _():
        to_next.wait_send()

    @pl.when(t > 0)
    def _():
        to_prev.wait_send()

    for d in range(peers):
        sib_copy(d).wait_send()
    for d in range(1, peers):
        mode_copy(d).wait_send()
        for upper in range(2):
            obj_copy(d, upper).wait_send()
    for d in range(1, chips):
        chip_copy(d).wait_send()
        ag_copy(d).wait_send()


def reduce(grad, pgrad, tiles, peers, half):
    modes, win = pgrad.shape[1:3]
    nm, hw = modes // peers, win // 2
    chips = tiles // 2
    rows = hw // chips
    tile_rows = grad.shape[1] - 2 * half
    cols = grad.shape[2]
    width = cols // peers
    dma = pltpu.SemaphoreType.DMA
    vmem = pl.BlockSpec(memory_space=pltpu.VMEM)
    return pl.pallas_call(
        functools.partial(reduce_kernel, tiles, peers, half),
        out_shape=(
            jax.ShapeDtypeStruct((2, tile_rows, width), F32),
            jax.ShapeDtypeStruct((2, nm, win, win), F32),
        ),
        in_specs=[vmem, vmem],
        out_specs=(vmem, vmem),
        scratch_shapes=[
            pltpu.VMEM((2, 2, half, cols), F32),
            pltpu.VMEM((peers, 2, nm, hw, win), F32),
            pltpu.VMEM((peers - 1, 2, nm, hw, win), F32),
            pltpu.VMEM((2, nm, hw, win), F32),
            pltpu.VMEM((chips - 1, 2, nm, rows, win), F32),
            pltpu.VMEM((peers - 1, 2, tile_rows, width), F32),
            dma((2,)), dma((2,)), dma((peers,)), dma((peers,)), dma((peers - 1,)), dma((peers - 1,)),
            dma((chips - 1,)), dma((chips - 1,)), dma((peers - 1, 2)), dma((peers - 1, 2)),
            dma((chips - 1,)), dma((chips - 1,)), dma((chips,)), dma((chips,)),
        ],
        compiler_params=pltpu.CompilerParams(
            collective_id=2, has_side_effects=True, vmem_limit_bytes=48 * MIB),
    )(grad, pgrad)


def body(object_field, probe_modes, measured, row_starts, col_starts, live_counts):
    tiles, peers = lax.axis_size("tile"), lax.axis_size("mode")
    half = probe_modes.shape[-1] // 2
    above, below, allp = gather(object_field, probe_modes, tiles, peers, half)
    me = jnp.stack([lax.axis_index("mode").astype(jnp.int32), jnp.int32(peers)])
    grad, pgrad = compute(row_starts, col_starts, live_counts, me, above, object_field, below, allp, measured, half)
    return reduce(grad, pgrad, tiles, peers, half)


def solution(mesh):
    return jax.shard_map(
        body,
        mesh=mesh,
        in_specs=(
            P(None, "tile", None),
            P(None, "mode", None, None),
            P("tile", None, None),
            P("tile"),
            P("tile"),
            P("tile"),
        ),
        out_specs=(P(None, "tile", "mode"), P(None, "mode", None, None)),
        check_vma=False,
    )
```

```python
import functools
import math

import jax
import jax.numpy as jnp
import numpy as np
from jax import lax
from jax.experimental import pallas as pl
from jax.experimental.pallas import tpu as pltpu
from jax.sharding import PartitionSpec as P

MESH = pl.DeviceIdType.MESH
MIB = 1024 * 1024
F32 = jnp.float32
BF16 = jnp.bfloat16


def dft_tables(window):
    index = np.arange(window)
    angles = (index[:, None] * index[None, :] % window) * (2.0 * math.pi / window)
    cr = np.cos(angles) / math.sqrt(window)
    ci = -np.sin(angles) / math.sqrt(window)
    left = np.block([[cr, -ci], [ci, cr]])
    right = np.block([[cr, ci], [-ci, cr]])
    return jnp.asarray(left, BF16), jnp.asarray(right, BF16)


def gather_kernel(tiles, peers, half, obj, prb, above, below, allp, halo_s, halo_r, prb_s, prb_r, fwd_s, fwd_r):
    t = lax.axis_index("tile")
    m = lax.axis_index("mode")
    sib = t + 1 - 2 * (t % 2)
    c = t % 2
    tile_rows = obj.shape[1]
    nm = prb.shape[1]
    win = prb.shape[2]
    hw = win // 2
    barrier = pltpu.get_barrier_semaphore()

    def hello(tt, mm):
        pl.semaphore_signal(barrier, inc=1, device_id=(tt, mm), device_id_type=MESH)

    @pl.when(t > 0)
    def _():
        hello(t - 1, m)

    @pl.when(t < tiles - 1)
    def _():
        hello(t + 1, m)

    for d in range(1, peers):
        hello(t, (m + d) % peers)
    pl.semaphore_wait(barrier, peers - 1 + (t + tiles - 1) // tiles + (2 * tiles - 2 - t) // tiles)

    def probe_copy(d, part):
        return pltpu.make_async_remote_copy(
            src_ref=prb.at[part, :, pl.ds(c * hw, hw)],
            dst_ref=allp.at[part, pl.ds(m * nm, nm), pl.ds(c * hw, hw)],
            send_sem=prb_s.at[d - 1, part],
            recv_sem=prb_r.at[d - 1, part],
            device_id=(t, (m + d) % peers),
            device_id_type=MESH,
        )

    def forward_copy(d, part, core):
        src = (m - d + peers) % peers
        view = allp.at[part, pl.ds(src * nm, nm), pl.ds(core * hw, hw)]
        return pltpu.make_async_remote_copy(
            src_ref=view,
            dst_ref=view,
            send_sem=fwd_s.at[d - 1, part],
            recv_sem=fwd_r.at[d - 1, part],
            device_id=(sib, m),
            device_id_type=MESH,
        )

    up = pltpu.make_async_remote_copy(
        src_ref=obj.at[:, pl.ds(tile_rows - half, half)], dst_ref=above,
        send_sem=halo_s.at[0], recv_sem=halo_r.at[0], device_id=(t + 1, m), device_id_type=MESH)
    down = pltpu.make_async_remote_copy(
        src_ref=obj.at[:, pl.ds(0, half)], dst_ref=below,
        send_sem=halo_s.at[1], recv_sem=halo_r.at[1], device_id=(t - 1, m), device_id_type=MESH)

    @pl.when(t < tiles - 1)
    def _():
        up.start()

    @pl.when(t > 0)
    def _():
        down.start()

    for d in range(1, peers):
        for part in range(2):
            probe_copy(d, part).start()
    for d in range(1, peers):
        for part in range(2):
            probe_copy(d, part).wait_recv()
            forward_copy(d, part, c).start()
    for d in range(1, peers):
        for part in range(2):
            forward_copy(d, part, 1 - c).wait_recv()
            forward_copy(d, part, c).wait_send()
            probe_copy(d, part).wait_send()

    @pl.when(t > 0)
    def _():
        up.wait_recv()
        down.wait_send()

    @pl.when(t < tiles - 1)
    def _():
        down.wait_recv()
        up.wait_send()


def gather(obj, prb, tiles, peers, half):
    cols = obj.shape[2]
    nm, win = prb.shape[1:3]
    dma = pltpu.SemaphoreType.DMA
    anyspace = pl.BlockSpec(memory_space=pl.ANY)
    return pl.pallas_call(
        functools.partial(gather_kernel, tiles, peers, half),
        out_shape=(
            jax.ShapeDtypeStruct((2, half, cols), F32),
            jax.ShapeDtypeStruct((2, half, cols), F32),
            jax.ShapeDtypeStruct((2, nm * peers, win, win), F32),
        ),
        in_specs=[anyspace, anyspace],
        out_specs=(anyspace, anyspace, anyspace),
        scratch_shapes=[dma((2,)), dma((2,)), dma((peers - 1, 2)), dma((peers - 1, 2)),
                        dma((peers - 1, 2)), dma((peers - 1, 2))],
        compiler_params=pltpu.CompilerParams(collective_id=1, has_side_effects=True),
    )(obj, prb)


def compute_kernel(half, peers, rows, cols, live, me, above, obj, below, allp, own, measured, left, right,
                   grad, pgrad, padded, prb, far, patch, terms, meas, sems, psems):
    m = me[0]
    nm = own.shape[1]
    win = patch.shape[1]
    tile_rows = obj.shape[1]
    modes = prb.shape[1]
    copies = [
        pltpu.make_async_copy(above, padded.at[:, pl.ds(0, half)], sems.at[0]),
        pltpu.make_async_copy(obj, padded.at[:, pl.ds(half, tile_rows)], sems.at[1]),
        pltpu.make_async_copy(below, padded.at[:, pl.ds(half + tile_rows, half)], sems.at[2]),
    ]
    copies.append(pltpu.make_async_copy(own, prb.at[:, pl.ds(m * nm, nm)], psems.at[0]))
    for d in range(1, peers):
        group = pl.ds((m + d) % peers * nm, nm)
        copies.append(pltpu.make_async_copy(allp.at[:, group], prb.at[:, group], psems.at[d]))
    for copy in copies:
        copy.start()
    grad[...] = jnp.zeros(grad.shape, F32)
    pgrad[...] = jnp.zeros(pgrad.shape, F32)
    for copy in copies:
        copy.wait()
    count = (live[0] - m + peers - 1) // peers

    def position(i, carry):
        slot = m + i * peers
        fetch = pltpu.make_async_copy(measured.at[slot], meas.at[0], sems.at[3])
        fetch.start()
        row = rows[slot] + half
        col = cols[slot]
        base = pl.multiple_of(jnp.minimum(col // 128, (padded.shape[2] - win - 128) // 128) * 128, 128)
        shift = col - base
        wide = win + 128
        tall = win + 8
        top = pl.multiple_of(jnp.minimum(row // 8, (padded.shape[1] - tall) // 8) * 8, 8)
        drop = row - top
        for part in range(2):
            block = padded[part, pl.ds(top, tall), pl.ds(base, wide)]
            block = pltpu.roll(block, (tall - drop) % tall, 0)[:win]
            patch[part] = pltpu.roll(block, (wide - shift) % wide, 1)[:, :win]
        meas[1] = jnp.zeros((win, win), F32)

        def forward(pair, carry):
            pr, pi = patch[0], patch[1]
            exits = []
            for k in range(2):
                qr, qi = prb[0, 2 * pair + k], prb[1, 2 * pair + k]
                er = (qr * pr - qi * pi).astype(BF16)
                ei = (qr * pi + qi * pr).astype(BF16)
                exits.append(jnp.concatenate([er, ei], axis=0))
            wave = jnp.concatenate(exits, axis=1)
            halfp = jnp.dot(left[...], wave, preferred_element_type=F32).astype(BF16)
            for k in range(2):
                lhs = jnp.concatenate(
                    [halfp[:win, k * win:(k + 1) * win], halfp[win:, k * win:(k + 1) * win]], axis=1)
                out = jnp.dot(lhs, right[...], preferred_element_type=F32)
                far[2 * pair + k] = out
                fr, fi = out[:, :win], out[:, win:]
                meas[1] += fr * fr + fi * fi
            return carry

        lax.fori_loop(0, modes // 2, forward, 0)
        fetch.wait()
        meas[1] = 1.0 - jnp.sqrt(meas[0]) / jnp.maximum(jnp.sqrt(meas[1]), 0.5)
        terms[...] = jnp.zeros(terms.shape, F32)

        def backward(pair, carry):
            scaling = meas[1]
            chis = []
            for k in range(2):
                value = far[2 * pair + k]
                chis.append(jnp.concatenate(
                    [(value[:, :win] * scaling).astype(BF16), (value[:, win:] * scaling).astype(BF16)], axis=0))
            wave = jnp.concatenate(chis, axis=1)
            halfp = jnp.dot(right[...], wave, preferred_element_type=F32).astype(BF16)
            for k in range(2):
                mode = 2 * pair + k
                lhs = jnp.concatenate(
                    [halfp[:win, k * win:(k + 1) * win], halfp[win:, k * win:(k + 1) * win]], axis=1)
                back = jnp.dot(lhs, left[...], preferred_element_type=F32)
                br, bi = back[:, :win], back[:, win:]
                pr, pi = patch[0], patch[1]
                qr, qi = prb[0, mode], prb[1, mode]
                terms[0, :win, :win] += qr * br + qi * bi
                terms[1, :win, :win] += qr * bi - qi * br
                pgrad[0, mode] += pr * br + pi * bi
                pgrad[1, mode] += pr * bi - pi * br
            return carry

        lax.fori_loop(0, modes // 2, backward, 0)
        for part in range(2):
            grad[part, pl.ds(top, tall), pl.ds(base, wide)] += pltpu.roll(pltpu.roll(terms[part], shift, 1), drop, 0)
        return carry

    lax.fori_loop(0, count, position, 0)


def compute(rows, cols, live, me, above, obj, below, allp, own, measured, half):
    modes, win = allp.shape[1:3]
    peers = modes // own.shape[1]
    left, right = dft_tables(win)
    anyspace = pl.BlockSpec(memory_space=pl.ANY)
    smem = pl.BlockSpec(memory_space=pltpu.SMEM)
    vmem = pl.BlockSpec(memory_space=pltpu.VMEM)
    height = obj.shape[1] + 2 * half
    return pl.pallas_call(
        functools.partial(compute_kernel, half, peers),
        out_shape=(
            jax.ShapeDtypeStruct((2, height, obj.shape[2]), F32),
            jax.ShapeDtypeStruct(allp.shape, F32),
        ),
        in_specs=[smem, smem, smem, smem, anyspace, anyspace, anyspace, anyspace, anyspace, anyspace, vmem, vmem],
        out_specs=(vmem, vmem),
        scratch_shapes=[
            pltpu.VMEM((2, height, obj.shape[2]), F32),
            pltpu.VMEM(allp.shape, F32),
            pltpu.VMEM((modes, win, 2 * win), F32),
            pltpu.VMEM((2, win, win), F32),
            pltpu.VMEM((2, win + 8, win + 128), F32),
            pltpu.VMEM((2, win, win), F32),
            pltpu.SemaphoreType.DMA((4,)),
            pltpu.SemaphoreType.DMA((peers,)),
        ],
        compiler_params=pltpu.CompilerParams(vmem_limit_bytes=48 * MIB),
    )(rows, cols, live, me, above, obj, below, allp, own, measured, left, right)


def reduce_kernel(tiles, peers, half, grad, pgrad, ograd, oprobe,
                  edge, sibp, modep, mine, nearp, farp, objp,
                  edge_s, edge_r, sib_s, sib_r, mode_s, mode_r, near_s, near_r, far_s, far_r,
                  obj_s, obj_r, back_near_s, back_near_r, back_far_s, back_far_r, fw_s, fw_r):
    t = lax.axis_index("tile")
    m = lax.axis_index("mode")
    c = t % 2
    lo = t // 2 % 2
    hi = t // 4
    highs = tiles // 4
    sib = t + 1 - 2 * c
    near = t + 2 - 4 * lo
    modes, win = pgrad.shape[1:3]
    nm = modes // peers
    hw = win // 2
    tile_rows = ograd.shape[1]
    width = ograd.shape[2]
    fine = hw // 2 // highs
    barrier = pltpu.get_barrier_semaphore()

    def hello(tt, mm):
        pl.semaphore_signal(barrier, inc=1, device_id=(tt, mm), device_id_type=MESH)

    def far_tile(d):
        return (hi + d) % highs * 4 + lo * 2 + c

    @pl.when(t > 0)
    def _():
        hello(t - 1, m)

    @pl.when(t < tiles - 1)
    def _():
        hello(t + 1, m)

    for d in range(1, peers):
        hello(t, (m + d) % peers)
    for d in range(1, highs):
        hello(far_tile(d), m)
    hello(near, m)
    pl.semaphore_wait(barrier, peers + highs - 1 + (t + tiles - 1) // tiles + (2 * tiles - 2 - t) // tiles)

    def remote(src, dst, ssem, rsem, tt, mm):
        return pltpu.make_async_remote_copy(
            src_ref=src, dst_ref=dst, send_sem=ssem, recv_sem=rsem,
            device_id=(tt, mm), device_id_type=MESH)

    to_next = remote(grad.at[:, pl.ds(half + tile_rows, half)], edge.at[0], edge_s.at[0], edge_r.at[0], t + 1, m)
    to_prev = remote(grad.at[:, pl.ds(0, half)], edge.at[1], edge_s.at[1], edge_r.at[1], t - 1, m)

    def sib_copy(d, part):
        group = ((m + d) % peers) * nm
        return remote(pgrad.at[part, pl.ds(group, nm), pl.ds((1 - c) * hw, hw)], sibp.at[d, part],
                      sib_s.at[d, part], sib_r.at[d, part], sib, m)

    def mode_copy(d, part):
        return remote(sibp.at[d, part], modep.at[d - 1, part],
                      mode_s.at[d - 1, part], mode_r.at[d - 1, part], t, (m + d) % peers)

    def obj_copy(d, upper):
        column = ((m + d) % peers) * width
        hr = tile_rows // 2
        return remote(grad.at[:, pl.ds(half + upper * hr, hr), pl.ds(column, width)],
                      objp.at[d - 1, :, pl.ds(upper * hr, hr)],
                      obj_s.at[d - 1, upper], obj_r.at[d - 1, upper], t, (m + d) % peers)

    def near_start(part, low, high):
        return low * (hw // 2) if part == 0 else high * 2 * fine + low * fine

    def far_start(part, low, high):
        return low * (hw // 2) + high * fine if part == 0 else high * 2 * fine

    near_rows = (hw // 2, fine)
    far_rows = (fine, 2 * fine)

    def near_copy(part):
        rows = near_rows[part]
        return remote(mine.at[part, :, pl.ds(near_start(part, 1 - lo, hi), rows)], nearp.at[part, :, pl.ds(0, rows)],
                      near_s.at[part], near_r.at[part], near, m)

    def far_copy(part, d):
        rows = far_rows[part]
        return remote(mine.at[part, :, pl.ds(far_start(part, lo, (hi + d) % highs), rows)],
                      farp.at[part, d - 1, :, pl.ds(0, rows)],
                      far_s.at[part, d - 1], far_r.at[part, d - 1], far_tile(d), m)

    def add_near(part):
        rows = near_rows[part]
        near_copy(part).wait_recv()
        mine[part, :, pl.ds(near_start(part, lo, hi), rows)] += nearp[part, :, pl.ds(0, rows)]

    def add_far(part):
        rows = far_rows[part]
        keep = pl.ds(far_start(part, lo, hi), rows)
        total = mine[part, :, keep]
        for d in range(1, highs):
            far_copy(part, d).wait_recv()
            total += farp[part, d - 1, :, pl.ds(0, rows)]
        mine[part, :, keep] = total

    def settle(part):
        start = lo * (hw // 2) + hi * fine if part == 0 else hi * 2 * fine + lo * fine
        oprobe[part, :, pl.ds(c * hw + start, fine)] = mine[part, :, pl.ds(start, fine)]

    def back_near(part):
        view = oprobe.at[part, :, pl.ds(c * hw + near_start(part, lo, hi), near_rows[part])]
        return remote(view, view, back_near_s.at[part], back_near_r.at[part], near, m)

    def back_far(part, d):
        view = oprobe.at[part, :, pl.ds(c * hw + far_start(part, lo, hi), far_rows[part])]
        return remote(view, view, back_far_s.at[part, d - 1], back_far_r.at[part, d - 1], far_tile(d), m)

    def fw_copy(part):
        view = oprobe.at[part, :, pl.ds(c * hw, hw)]
        return remote(view, view, fw_s.at[part], fw_r.at[part], sib, m)

    for part in range(2):
        for d in range(1, peers):
            sib_copy(d, part).start()
    for part in range(2):
        sib_copy(0, part).start()

    @pl.when(t < tiles - 1)
    def _():
        to_next.start()

    @pl.when(t > 0)
    def _():
        to_prev.start()

    for part in range(2):
        for d in range(1, peers):
            group = ((m + d) % peers) * nm
            sib_copy(d, part).wait_recv()
            sibp[d, part] += pgrad[part, pl.ds(group, nm), pl.ds(c * hw, hw)]
            mode_copy(d, part).start()
    for part in range(2):
        sib_copy(0, part).wait_recv()
        mine[part] = sibp[0, part] + pgrad[part, pl.ds(m * nm, nm), pl.ds(c * hw, hw)]

    for d in range(1, peers):
        mode_copy(d, 0).wait_recv()
        mine[0] += modep[d - 1, 0]
    near_copy(0).start()

    @pl.when(t > 0)
    def _():
        to_next.wait_recv()
        grad[:, pl.ds(half, half)] += edge[0]

    for d in range(1, peers):
        obj_copy(d, 0).start()

    @pl.when(t < tiles - 1)
    def _():
        to_prev.wait_recv()
        grad[:, pl.ds(tile_rows, half)] += edge[1]

    for d in range(1, peers):
        obj_copy(d, 1).start()
    for d in range(1, peers):
        mode_copy(d, 1).wait_recv()
        mine[1] += modep[d - 1, 1]
    for d in range(1, highs):
        far_copy(1, d).start()
    add_near(0)
    for d in range(1, highs):
        far_copy(0, d).start()
    add_far(1)
    near_copy(1).start()
    add_far(0)
    settle(0)
    for d in range(1, highs):
        back_far(0, d).start()
    add_near(1)
    settle(1)
    back_near(1).start()
    for d in range(1, highs):
        back_far(0, d).wait_recv()
    back_near(0).start()
    back_near(1).wait_recv()
    for d in range(1, highs):
        back_far(1, d).start()

    ograd[...] = grad[:, pl.ds(half, tile_rows), pl.ds(pl.multiple_of(m * width, 128), width)]
    back_near(0).wait_recv()
    fw_copy(0).start()
    for d in range(1, highs):
        back_far(1, d).wait_recv()
    fw_copy(1).start()
    for d in range(1, peers):
        for upper in range(2):
            obj_copy(d, upper).wait_recv()
        ograd[...] += objp[d - 1]
    for part in range(2):
        fw_copy(part).wait_recv()

    @pl.when(t < tiles - 1)
    def _():
        to_next.wait_send()

    @pl.when(t > 0)
    def _():
        to_prev.wait_send()

    for part in range(2):
        fw_copy(part).wait_send()
        near_copy(part).wait_send()
        back_near(part).wait_send()
        for d in range(peers):
            sib_copy(d, part).wait_send()
        for d in range(1, peers):
            mode_copy(d, part).wait_send()
            obj_copy(d, part).wait_send()
        for d in range(1, highs):
            far_copy(part, d).wait_send()
            back_far(part, d).wait_send()


def reduce(grad, pgrad, tiles, peers, half):
    modes, win = pgrad.shape[1:3]
    nm, hw = modes // peers, win // 2
    highs = tiles // 4
    tile_rows = grad.shape[1] - 2 * half
    cols = grad.shape[2]
    width = cols // peers
    dma = pltpu.SemaphoreType.DMA
    vmem = pl.BlockSpec(memory_space=pltpu.VMEM)
    return pl.pallas_call(
        functools.partial(reduce_kernel, tiles, peers, half),
        out_shape=(
            jax.ShapeDtypeStruct((2, tile_rows, width), F32),
            jax.ShapeDtypeStruct((2, nm, win, win), F32),
        ),
        in_specs=[vmem, vmem],
        out_specs=(vmem, vmem),
        scratch_shapes=[
            pltpu.VMEM((2, 2, half, cols), F32),
            pltpu.VMEM((peers, 2, nm, hw, win), F32),
            pltpu.VMEM((peers - 1, 2, nm, hw, win), F32),
            pltpu.VMEM((2, nm, hw, win), F32),
            pltpu.VMEM((2, nm, hw // 2, win), F32),
            pltpu.VMEM((2, highs - 1, nm, hw // highs, win), F32),
            pltpu.VMEM((peers - 1, 2, tile_rows, width), F32),
            dma((2,)), dma((2,)), dma((peers, 2)), dma((peers, 2)), dma((peers - 1, 2)), dma((peers - 1, 2)),
            dma((2,)), dma((2,)), dma((2, highs - 1)), dma((2, highs - 1)),
            dma((peers - 1, 2)), dma((peers - 1, 2)),
            dma((2,)), dma((2,)), dma((2, highs - 1)), dma((2, highs - 1)), dma((2,)), dma((2,)),
        ],
        compiler_params=pltpu.CompilerParams(
            collective_id=2, has_side_effects=True, vmem_limit_bytes=48 * MIB),
    )(grad, pgrad)


def body(object_field, probe_modes, measured, row_starts, col_starts, live_counts):
    tiles, peers = lax.axis_size("tile"), lax.axis_size("mode")
    half = probe_modes.shape[-1] // 2
    above, below, allp = gather(object_field, probe_modes, tiles, peers, half)
    me = lax.axis_index("mode").astype(jnp.int32).reshape(1)
    grad, pgrad = compute(row_starts, col_starts, live_counts, me, above, object_field, below, allp, probe_modes, measured, half)
    return reduce(grad, pgrad, tiles, peers, half)


def solution(mesh):
    return jax.shard_map(
        body,
        mesh=mesh,
        in_specs=(
            P(None, "tile", None),
            P(None, "mode", None, None),
            P("tile", None, None),
            P("tile"),
            P("tile"),
            P("tile"),
        ),
        out_specs=(P(None, "tile", "mode"), P(None, "mode", None, None)),
        check_vma=False,
    )
```

```python
import functools
import math

import jax
import jax.numpy as jnp
import numpy as np
from jax import lax
from jax.experimental import pallas as pl
from jax.experimental.pallas import tpu as pltpu
from jax.sharding import PartitionSpec as P

MESH = pl.DeviceIdType.MESH
MIB = 1024 * 1024
F32 = jnp.float32
BF16 = jnp.bfloat16


def dft_tables(window):
    index = np.arange(window)
    angles = (index[:, None] * index[None, :] % window) * (2.0 * math.pi / window)
    cr = np.cos(angles) / math.sqrt(window)
    ci = -np.sin(angles) / math.sqrt(window)
    left = np.block([[cr, -ci], [ci, cr]])
    right = np.block([[cr, ci], [-ci, cr]])
    return jnp.asarray(left, BF16), jnp.asarray(right, BF16)


def gather_kernel(tiles, peers, half, obj, prb, above, below, allp, halo_s, halo_r, prb_s, prb_r, fwd_s, fwd_r):
    t = lax.axis_index("tile")
    m = lax.axis_index("mode")
    sib = t + 1 - 2 * (t % 2)
    c = t % 2
    tile_rows = obj.shape[1]
    nm = prb.shape[1]
    win = prb.shape[2]
    hw = win // 2
    barrier = pltpu.get_barrier_semaphore()

    def hello(tt, mm):
        pl.semaphore_signal(barrier, inc=1, device_id=(tt, mm), device_id_type=MESH)

    @pl.when(t > 0)
    def _():
        hello(t - 1, m)

    @pl.when(t < tiles - 1)
    def _():
        hello(t + 1, m)

    for d in range(1, peers):
        hello(t, (m + d) % peers)
    pl.semaphore_wait(barrier, peers - 1 + (t + tiles - 1) // tiles + (2 * tiles - 2 - t) // tiles)

    def probe_copy(d, part):
        return pltpu.make_async_remote_copy(
            src_ref=prb.at[part, :, pl.ds(c * hw, hw)],
            dst_ref=allp.at[part, pl.ds(m * nm, nm), pl.ds(c * hw, hw)],
            send_sem=prb_s.at[d - 1, part],
            recv_sem=prb_r.at[d - 1, part],
            device_id=(t, (m + d) % peers),
            device_id_type=MESH,
        )

    def forward_copy(d, part, core):
        src = (m - d + peers) % peers
        view = allp.at[part, pl.ds(src * nm, nm), pl.ds(core * hw, hw)]
        return pltpu.make_async_remote_copy(
            src_ref=view,
            dst_ref=view,
            send_sem=fwd_s.at[d - 1, part],
            recv_sem=fwd_r.at[d - 1, part],
            device_id=(sib, m),
            device_id_type=MESH,
        )

    up = pltpu.make_async_remote_copy(
        src_ref=obj.at[:, pl.ds(tile_rows - half, half)], dst_ref=above,
        send_sem=halo_s.at[0], recv_sem=halo_r.at[0], device_id=(t + 1, m), device_id_type=MESH)
    down = pltpu.make_async_remote_copy(
        src_ref=obj.at[:, pl.ds(0, half)], dst_ref=below,
        send_sem=halo_s.at[1], recv_sem=halo_r.at[1], device_id=(t - 1, m), device_id_type=MESH)

    @pl.when(t < tiles - 1)
    def _():
        up.start()

    @pl.when(t > 0)
    def _():
        down.start()

    for d in range(1, peers):
        for part in range(2):
            probe_copy(d, part).start()
    for d in range(1, peers):
        for part in range(2):
            probe_copy(d, part).wait_recv()
            forward_copy(d, part, c).start()
    for d in range(1, peers):
        for part in range(2):
            forward_copy(d, part, 1 - c).wait_recv()
            forward_copy(d, part, c).wait_send()
            probe_copy(d, part).wait_send()

    @pl.when(t > 0)
    def _():
        up.wait_recv()
        down.wait_send()

    @pl.when(t < tiles - 1)
    def _():
        down.wait_recv()
        up.wait_send()


def gather(obj, prb, tiles, peers, half):
    cols = obj.shape[2]
    nm, win = prb.shape[1:3]
    dma = pltpu.SemaphoreType.DMA
    anyspace = pl.BlockSpec(memory_space=pl.ANY)
    return pl.pallas_call(
        functools.partial(gather_kernel, tiles, peers, half),
        out_shape=(
            jax.ShapeDtypeStruct((2, half, cols), F32),
            jax.ShapeDtypeStruct((2, half, cols), F32),
            jax.ShapeDtypeStruct((2, nm * peers, win, win), F32),
        ),
        in_specs=[anyspace, anyspace],
        out_specs=(anyspace, anyspace, anyspace),
        scratch_shapes=[dma((2,)), dma((2,)), dma((peers - 1, 2)), dma((peers - 1, 2)),
                        dma((peers - 1, 2)), dma((peers - 1, 2))],
        compiler_params=pltpu.CompilerParams(collective_id=1, has_side_effects=True),
    )(obj, prb)


def compute_kernel(half, peers, rows, cols, live, me, above, obj, below, allp, own, measured, left, right,
                   grad, pgrad, padded, prb, far, patch, terms, meas, sems, psems):
    m = me[0]
    nm = own.shape[1]
    win = patch.shape[1]
    tile_rows = obj.shape[1]
    modes = prb.shape[1]
    copies = [
        pltpu.make_async_copy(above, padded.at[:, pl.ds(0, half)], sems.at[0]),
        pltpu.make_async_copy(obj, padded.at[:, pl.ds(half, tile_rows)], sems.at[1]),
        pltpu.make_async_copy(below, padded.at[:, pl.ds(half + tile_rows, half)], sems.at[2]),
    ]
    copies.append(pltpu.make_async_copy(own, prb.at[:, pl.ds(m * nm, nm)], psems.at[0]))
    for d in range(1, peers):
        group = pl.ds((m + d) % peers * nm, nm)
        copies.append(pltpu.make_async_copy(allp.at[:, group], prb.at[:, group], psems.at[d]))
    for copy in copies:
        copy.start()
    grad[...] = jnp.zeros(grad.shape, F32)
    pgrad[...] = jnp.zeros(pgrad.shape, F32)
    for copy in copies:
        copy.wait()
    count = (live[0] - m + peers - 1) // peers

    batch, groups = 2, modes // 2

    def twice(rows_table, wave, cols_table):
        halfp = jnp.dot(rows_table, wave, preferred_element_type=F32).astype(BF16)
        parts = [
            jnp.concatenate([halfp[:win, k * win:(k + 1) * win], halfp[win:, k * win:(k + 1) * win]], axis=1)
            for k in range(batch)
        ]
        return [jnp.dot(part, cols_table, preferred_element_type=F32) for part in parts]

    def position(i, carry):
        slot = m + i * peers
        fetch = pltpu.make_async_copy(measured.at[slot], meas.at[0], sems.at[3])
        fetch.start()
        row = rows[slot] + half
        col = cols[slot]
        base = pl.multiple_of(jnp.minimum(col // 128, (padded.shape[2] - win - 128) // 128) * 128, 128)
        shift = col - base
        wide = win + 128
        tall = win + 8
        top = pl.multiple_of(jnp.minimum(row // 8, (padded.shape[1] - tall) // 8) * 8, 8)
        drop = row - top
        for part in range(2):
            block = padded[part, pl.ds(top, tall), pl.ds(base, wide)]
            block = pltpu.roll(block, (tall - drop) % tall, 0)[:win]
            patch[part] = pltpu.roll(block, (wide - shift) % wide, 1)[:, :win]
        meas[1] = jnp.zeros((win, win), F32)

        def forward(step, carry):
            for g in range(groups):
                first = (step * groups + g) * batch
                pr, pi = patch[0], patch[1]
                exits = []
                for k in range(batch):
                    qr, qi = prb[0, first + k], prb[1, first + k]
                    er = (qr * pr - qi * pi).astype(BF16)
                    ei = (qr * pi + qi * pr).astype(BF16)
                    exits.append(jnp.concatenate([er, ei], axis=0))
                outs = twice(left[...], jnp.concatenate(exits, axis=1), right[...])
                total = meas[1]
                for k in range(batch):
                    far[first + k] = outs[k]
                    fr, fi = outs[k][:, :win], outs[k][:, win:]
                    total += fr * fr + fi * fi
                meas[1] = total
            return carry

        lax.fori_loop(0, modes // (batch * groups), forward, 0)
        fetch.wait()
        meas[1] = 1.0 - jnp.sqrt(meas[0]) / jnp.maximum(jnp.sqrt(meas[1]), 0.5)
        terms[...] = jnp.zeros(terms.shape, F32)

        def backward(step, carry):
            for g in range(groups):
                first = (step * groups + g) * batch
                scaling = meas[1]
                chis = []
                for k in range(batch):
                    value = far[first + k]
                    chis.append(jnp.concatenate(
                        [(value[:, :win] * scaling).astype(BF16), (value[:, win:] * scaling).astype(BF16)], axis=0))
                outs = twice(right[...], jnp.concatenate(chis, axis=1), left[...])
                pr, pi = patch[0], patch[1]
                tr, ti = terms[0, :win, :win], terms[1, :win, :win]
                for k in range(batch):
                    br, bi = outs[k][:, :win], outs[k][:, win:]
                    qr, qi = prb[0, first + k], prb[1, first + k]
                    tr += qr * br + qi * bi
                    ti += qr * bi - qi * br
                    pgrad[0, first + k] += pr * br + pi * bi
                    pgrad[1, first + k] += pr * bi - pi * br
                terms[0, :win, :win] = tr
                terms[1, :win, :win] = ti
            return carry

        lax.fori_loop(0, modes // (batch * groups), backward, 0)
        for part in range(2):
            grad[part, pl.ds(top, tall), pl.ds(base, wide)] += pltpu.roll(pltpu.roll(terms[part], shift, 1), drop, 0)
        return carry

    lax.fori_loop(0, count, position, 0)


def compute(rows, cols, live, me, above, obj, below, allp, own, measured, half):
    modes, win = allp.shape[1:3]
    peers = modes // own.shape[1]
    left, right = dft_tables(win)
    anyspace = pl.BlockSpec(memory_space=pl.ANY)
    smem = pl.BlockSpec(memory_space=pltpu.SMEM)
    vmem = pl.BlockSpec(memory_space=pltpu.VMEM)
    height = obj.shape[1] + 2 * half
    return pl.pallas_call(
        functools.partial(compute_kernel, half, peers),
        out_shape=(
            jax.ShapeDtypeStruct((2, height, obj.shape[2]), F32),
            jax.ShapeDtypeStruct(allp.shape, F32),
        ),
        in_specs=[smem, smem, smem, smem, anyspace, anyspace, anyspace, anyspace, anyspace, anyspace, vmem, vmem],
        out_specs=(vmem, vmem),
        scratch_shapes=[
            pltpu.VMEM((2, height, obj.shape[2]), F32),
            pltpu.VMEM(allp.shape, F32),
            pltpu.VMEM((modes, win, 2 * win), F32),
            pltpu.VMEM((2, win, win), F32),
            pltpu.VMEM((2, win + 8, win + 128), F32),
            pltpu.VMEM((2, win, win), F32),
            pltpu.SemaphoreType.DMA((4,)),
            pltpu.SemaphoreType.DMA((peers,)),
        ],
        compiler_params=pltpu.CompilerParams(vmem_limit_bytes=48 * MIB),
    )(rows, cols, live, me, above, obj, below, allp, own, measured, left, right)


def reduce_kernel(tiles, peers, half, grad, pgrad, ograd, oprobe,
                  inner, ours, edge, sibp, modep, mine, nearp, farp, objp, load,
                  edge_s, edge_r, sib_s, sib_r, mode_s, mode_r, near_s, near_r, far_s, far_r,
                  obj_s, obj_r, back_near_s, back_near_r, back_far_s, back_far_r, fw_s, fw_r):
    t = lax.axis_index("tile")
    m = lax.axis_index("mode")
    c = t % 2
    lo = t // 2 % 2
    hi = t // 4
    highs = tiles // 4
    sib = t + 1 - 2 * c
    near = t + 2 - 4 * lo
    modes, win = pgrad.shape[1:3]
    nm = modes // peers
    hw = win // 2
    tile_rows = ograd.shape[1]
    width = ograd.shape[2]
    fine = hw // 2 // highs
    barrier = pltpu.get_barrier_semaphore()

    def hello(tt, mm):
        pl.semaphore_signal(barrier, inc=1, device_id=(tt, mm), device_id_type=MESH)

    def far_tile(d):
        return (hi + d) % highs * 4 + lo * 2 + c

    @pl.when(t > 0)
    def _():
        hello(t - 1, m)

    @pl.when(t < tiles - 1)
    def _():
        hello(t + 1, m)

    for d in range(1, peers):
        hello(t, (m + d) % peers)
    for d in range(1, highs):
        hello(far_tile(d), m)
    hello(near, m)
    pl.semaphore_wait(barrier, peers + highs - 1 + (t + tiles - 1) // tiles + (2 * tiles - 2 - t) // tiles)

    fetch_inner = pltpu.make_async_copy(grad.at[:, pl.ds(half, tile_rows)], inner, load.at[0])
    fetch_ours = pltpu.make_async_copy(pgrad.at[:, :, pl.ds(c * hw, hw)], ours, load.at[1])

    def remote(src, dst, ssem, rsem, tt, mm):
        return pltpu.make_async_remote_copy(
            src_ref=src, dst_ref=dst, send_sem=ssem, recv_sem=rsem,
            device_id=(tt, mm), device_id_type=MESH)

    to_next = remote(grad.at[:, pl.ds(half + tile_rows, half)], edge.at[0], edge_s.at[0], edge_r.at[0], t + 1, m)
    to_prev = remote(grad.at[:, pl.ds(0, half)], edge.at[1], edge_s.at[1], edge_r.at[1], t - 1, m)

    def sib_copy(d, part):
        group = ((m + d) % peers) * nm
        return remote(pgrad.at[part, pl.ds(group, nm), pl.ds((1 - c) * hw, hw)], sibp.at[d, part],
                      sib_s.at[d, part], sib_r.at[d, part], sib, m)

    def mode_copy(d, part):
        return remote(sibp.at[d, part], modep.at[d - 1, part],
                      mode_s.at[d - 1, part], mode_r.at[d - 1, part], t, (m + d) % peers)

    def obj_copy(d, upper):
        column = ((m + d) % peers) * width
        hr = tile_rows // 2
        return remote(inner.at[:, pl.ds(upper * hr, hr), pl.ds(column, width)],
                      objp.at[d - 1, :, pl.ds(upper * hr, hr)],
                      obj_s.at[d - 1, upper], obj_r.at[d - 1, upper], t, (m + d) % peers)

    def near_start(part, low, high):
        return low * (hw // 2) if part == 0 else high * 2 * fine + low * fine

    def far_start(part, low, high):
        return low * (hw // 2) + high * fine if part == 0 else high * 2 * fine

    near_rows = (hw // 2, fine)
    far_rows = (fine, 2 * fine)

    def near_copy(part):
        rows = near_rows[part]
        return remote(mine.at[part, :, pl.ds(near_start(part, 1 - lo, hi), rows)], nearp.at[part, :, pl.ds(0, rows)],
                      near_s.at[part], near_r.at[part], near, m)

    def far_copy(part, d):
        rows = far_rows[part]
        return remote(mine.at[part, :, pl.ds(far_start(part, lo, (hi + d) % highs), rows)],
                      farp.at[part, d - 1, :, pl.ds(0, rows)],
                      far_s.at[part, d - 1], far_r.at[part, d - 1], far_tile(d), m)

    def add_near(part):
        rows = near_rows[part]
        near_copy(part).wait_recv()
        mine[part, :, pl.ds(near_start(part, lo, hi), rows)] += nearp[part, :, pl.ds(0, rows)]

    def add_far(part):
        rows = far_rows[part]
        keep = pl.ds(far_start(part, lo, hi), rows)
        total = mine[part, :, keep]
        for d in range(1, highs):
            far_copy(part, d).wait_recv()
            total += farp[part, d - 1, :, pl.ds(0, rows)]
        mine[part, :, keep] = total

    def settle(part):
        start = lo * (hw // 2) + hi * fine if part == 0 else hi * 2 * fine + lo * fine
        oprobe[part, :, pl.ds(c * hw + start, fine)] = mine[part, :, pl.ds(start, fine)]

    def back_near(part):
        view = oprobe.at[part, :, pl.ds(c * hw + near_start(part, lo, hi), near_rows[part])]
        return remote(view, view, back_near_s.at[part], back_near_r.at[part], near, m)

    def back_far(part, d):
        view = oprobe.at[part, :, pl.ds(c * hw + far_start(part, lo, hi), far_rows[part])]
        return remote(view, view, back_far_s.at[part, d - 1], back_far_r.at[part, d - 1], far_tile(d), m)

    def fw_copy(part):
        view = oprobe.at[part, :, pl.ds(c * hw, hw)]
        return remote(view, view, fw_s.at[part], fw_r.at[part], sib, m)

    for part in range(2):
        for d in range(1, peers):
            sib_copy(d, part).start()
    for part in range(2):
        sib_copy(0, part).start()

    @pl.when(t < tiles - 1)
    def _():
        to_next.start()

    @pl.when(t > 0)
    def _():
        to_prev.start()

    fetch_ours.start()
    fetch_inner.start()
    fetch_ours.wait()
    for part in range(2):
        for d in range(1, peers):
            group = ((m + d) % peers) * nm
            sib_copy(d, part).wait_recv()
            sibp[d, part] += ours[part, pl.ds(group, nm)]
            mode_copy(d, part).start()
    for part in range(2):
        sib_copy(0, part).wait_recv()
        mine[part] = sibp[0, part] + ours[part, pl.ds(m * nm, nm)]
    fetch_inner.wait()

    for d in range(1, peers):
        mode_copy(d, 0).wait_recv()
        mine[0] += modep[d - 1, 0]
    near_copy(0).start()

    @pl.when(t > 0)
    def _():
        to_next.wait_recv()
        inner[:, pl.ds(0, half)] += edge[0]

    for d in range(1, peers):
        obj_copy(d, 0).start()

    @pl.when(t < tiles - 1)
    def _():
        to_prev.wait_recv()
        inner[:, pl.ds(tile_rows - half, half)] += edge[1]

    for d in range(1, peers):
        obj_copy(d, 1).start()
    for d in range(1, peers):
        mode_copy(d, 1).wait_recv()
        mine[1] += modep[d - 1, 1]
    for d in range(1, highs):
        far_copy(1, d).start()
    add_near(0)
    for d in range(1, highs):
        far_copy(0, d).start()
    add_far(1)
    near_copy(1).start()
    add_far(0)
    settle(0)
    for d in range(1, highs):
        back_far(0, d).start()
    add_near(1)
    settle(1)
    back_near(1).start()
    for d in range(1, highs):
        back_far(0, d).wait_recv()
    back_near(0).start()
    back_near(1).wait_recv()
    for d in range(1, highs):
        back_far(1, d).start()

    ograd[...] = inner[:, :, pl.ds(pl.multiple_of(m * width, 128), width)]
    back_near(0).wait_recv()
    fw_copy(0).start()
    for d in range(1, highs):
        back_far(1, d).wait_recv()
    fw_copy(1).start()
    for d in range(1, peers):
        for upper in range(2):
            obj_copy(d, upper).wait_recv()
        ograd[...] += objp[d - 1]
    for part in range(2):
        fw_copy(part).wait_recv()

    @pl.when(t < tiles - 1)
    def _():
        to_next.wait_send()

    @pl.when(t > 0)
    def _():
        to_prev.wait_send()

    for part in range(2):
        fw_copy(part).wait_send()
        near_copy(part).wait_send()
        back_near(part).wait_send()
        for d in range(peers):
            sib_copy(d, part).wait_send()
        for d in range(1, peers):
            mode_copy(d, part).wait_send()
            obj_copy(d, part).wait_send()
        for d in range(1, highs):
            far_copy(part, d).wait_send()
            back_far(part, d).wait_send()


def reduce(grad, pgrad, tiles, peers, half):
    modes, win = pgrad.shape[1:3]
    nm, hw = modes // peers, win // 2
    highs = tiles // 4
    tile_rows = grad.shape[1] - 2 * half
    cols = grad.shape[2]
    width = cols // peers
    dma = pltpu.SemaphoreType.DMA
    vmem = pl.BlockSpec(memory_space=pltpu.VMEM)
    anyspace = pl.BlockSpec(memory_space=pl.ANY)
    return pl.pallas_call(
        functools.partial(reduce_kernel, tiles, peers, half),
        out_shape=(
            jax.ShapeDtypeStruct((2, tile_rows, width), F32),
            jax.ShapeDtypeStruct((2, nm, win, win), F32),
        ),
        in_specs=[anyspace, anyspace],
        out_specs=(vmem, vmem),
        scratch_shapes=[
            pltpu.VMEM((2, tile_rows, cols), F32),
            pltpu.VMEM((2, modes, hw, win), F32),
            pltpu.VMEM((2, 2, half, cols), F32),
            pltpu.VMEM((peers, 2, nm, hw, win), F32),
            pltpu.VMEM((peers - 1, 2, nm, hw, win), F32),
            pltpu.VMEM((2, nm, hw, win), F32),
            pltpu.VMEM((2, nm, hw // 2, win), F32),
            pltpu.VMEM((2, highs - 1, nm, hw // highs, win), F32),
            pltpu.VMEM((peers - 1, 2, tile_rows, width), F32),
            dma((2,)), dma((2,)), dma((2,)), dma((peers, 2)), dma((peers, 2)), dma((peers - 1, 2)), dma((peers - 1, 2)),
            dma((2,)), dma((2,)), dma((2, highs - 1)), dma((2, highs - 1)),
            dma((peers - 1, 2)), dma((peers - 1, 2)),
            dma((2,)), dma((2,)), dma((2, highs - 1)), dma((2, highs - 1)), dma((2,)), dma((2,)),
        ],
        compiler_params=pltpu.CompilerParams(
            collective_id=2, has_side_effects=True, vmem_limit_bytes=48 * MIB),
    )(grad, pgrad)


def body(object_field, probe_modes, measured, row_starts, col_starts, live_counts):
    tiles, peers = lax.axis_size("tile"), lax.axis_size("mode")
    half = probe_modes.shape[-1] // 2
    above, below, allp = gather(object_field, probe_modes, tiles, peers, half)
    me = lax.axis_index("mode").astype(jnp.int32).reshape(1)
    grad, pgrad = compute(row_starts, col_starts, live_counts, me, above, object_field, below, allp, probe_modes, measured, half)
    return reduce(grad, pgrad, tiles, peers, half)


def solution(mesh):
    return jax.shard_map(
        body,
        mesh=mesh,
        in_specs=(
            P(None, "tile", None),
            P(None, "mode", None, None),
            P("tile", None, None),
            P("tile"),
            P("tile"),
            P("tile"),
        ),
        out_specs=(P(None, "tile", "mode"), P(None, "mode", None, None)),
        check_vma=False,
    )
```
